32 devices in a mesh: parts: 2 (over x), section: 16 (over z, y, core).
Axes of the slice: x: 2, y: 2, z: 4, core: 2. Of those that a mesh axis runs over, the one named last changes fastest.
Arguments:
- activations: bfloat16 [16, 256, 4, 4096], P('section', 'parts'), parts along dimension 1, may hold values from -6 to 6
- out_grads: bfloat16 [16, 256, 4, 1024], P('section', 'parts'), parts along dimension 1, may hold values from -6 to 6
- in_proj: bfloat16 [16, 16, 4096], P('section'), as said below
- out_proj: bfloat16 [16, 16, 1024], P('section'), as said below
- queries: bfloat16 [16, 256, 256], P('section'), as said below
- assignment: int32 [256], P('parts'), parts along dimension 0, may hold values from 0 to 127, each once
Outputs:
- scores: float32 [256, 256], P(('parts', 'section')), parts along dimension 0
The draws below stay inside these ranges and needn't reach their ends.
There are 2 independent parts, one for each index of `parts`. The reference program is written for one: setup_inputs(seed, part) draws one part's arguments, and reference() takes and returns one part's arrays. A program takes and returns all parts, laid end to end along the dimension named above; an argument that names none is the same for every part. Nothing has to cross between parts.
Inputs may be any that keep to these rules, and one draw needn't show every extreme that they name: `assignment`: a permutation of the 128 examples. `in_proj`: entries at indices that differ by a multiple of 16 are equal. `out_proj`: entries at indices that differ by a multiple of 16 are equal. `queries`: entries at indices that differ by a multiple of 16 are equal.
All inputs are finite; a program needn't handle non-finite values.
Results may differ from the reference program's by a relative error of at most 0.01.
Values may be sent and summed in bfloat16 or wider, within the bound.
A program may use at most 64 MiB of HBM per device.

```python
import jax
import jax.numpy as jnp
from jax import lax

D_IN = 4096
D_OUT = 1024
K_IN = 16
K_OUT = 16
TOK = 4
QB = 128
LAYERS = 16
GROUPS = 1
EX_G = 128
EX = 128
KF = 256
FEAT = 4096


def tiled_normal(key, shape, scale):
    layer_draw = jnp.clip(jax.random.normal(key, shape, jnp.float32), -6.0, 6.0) * scale
    return jnp.tile(layer_draw, (GROUPS, 1, 1))


def draw_in_proj(key, part):
    key = jax.random.fold_in(key, 1)
    return tiled_normal(key, (LAYERS, K_IN, D_IN), D_IN ** (-0.5)).astype(jnp.bfloat16)


def draw_out_proj(key, part):
    key = jax.random.fold_in(key, 2)
    return tiled_normal(key, (LAYERS, K_OUT, D_OUT), D_OUT ** (-0.5)).astype(jnp.bfloat16)


def draw_queries(key, part):
    key = jax.random.fold_in(key, 3)
    return tiled_normal(key, (LAYERS, 2 * QB, KF), 1.0).astype(jnp.bfloat16)


def block_scale(stream_key, dims, pieces, low, top_value):
    def one(dim, shards_of):
        heights = jax.random.uniform(jax.random.fold_in(jax.random.fold_in(stream_key, 6), dim), (shards_of,), jnp.float32, low / len(pieces), top_value / len(pieces))
        return jnp.repeat(jnp.exp(heights), dims[dim] // shards_of).reshape((-1,) + (1,) * (len(dims) - dim - 1))

    factor_of = one(*pieces[0])
    for cut in pieces[1:]:
        factor_of = factor_of * one(*cut)
    return factor_of


def scatter_about(key, dims, deviation, most, shards=(), held_as=jnp.bfloat16):
    array = jax.random.normal(key, dims, jnp.float32) * deviation
    if len(shards) > 0:
        array = block_scale(key, dims, shards, -0.22, 0.18) * array
    return jnp.clip(array, min=-most, max=most).astype(held_as)


def setup_inputs(seed: int = 0, part: int = 0) -> dict:
    key_list = jax.random.split(jax.random.key(seed), 7)
    part_splits = jax.random.split(jax.random.fold_in(key_list[6], part), 7)
    activations = scatter_about(part_splits[0], (LAYERS * GROUPS, EX_G, TOK, D_IN), 1.0, 6.0, ((0, 16),))
    out_grads = scatter_about(part_splits[1], (LAYERS * GROUPS, EX_G, TOK, D_OUT), 1.0, 6.0, ((0, 16),))
    in_proj = draw_in_proj(jax.random.fold_in(key_list[6], 71), part)
    out_proj = draw_out_proj(jax.random.fold_in(key_list[6], 71), part)
    queries = draw_queries(jax.random.fold_in(key_list[6], 71), part)
    assignment = jax.random.permutation(part_splits[5], EX).astype(jnp.int32)
    return {"activations": activations, "out_grads": out_grads, "in_proj": in_proj, "out_proj": out_proj, "queries": queries, "assignment": assignment}


def slot_features(bundle):
    layer_acts, layer_grads, in_weight, out_weight = bundle
    act_proj = jnp.einsum('etd,kd->etk', layer_acts.astype(jnp.float32), in_weight.astype(jnp.float32))
    grad_proj = jnp.einsum('etd,kd->etk', layer_grads.astype(jnp.float32), out_weight.astype(jnp.float32))
    outer_sum = jnp.einsum('eta,etb->eab', grad_proj, act_proj)
    return outer_sum.reshape(outer_sum.shape[0], -1).astype(jnp.bfloat16)

def reference(activations, out_grads, in_proj, out_proj, queries, assignment):
    per_slot = lax.map(slot_features, (activations, out_grads, in_proj, out_proj))
    grouped = per_slot.reshape(GROUPS, LAYERS, EX_G, KF)
    features = jnp.transpose(grouped, (0, 2, 1, 3)).reshape(EX, FEAT)
    query_matrix = jnp.transpose(queries[:LAYERS], (1, 0, 2)).reshape(2 * QB, FEAT)
    widened = features.astype(jnp.float32)
    inv_norm = lax.rsqrt(lax.optimization_barrier(jnp.sum(widened * widened, axis=1)) + 1e-06)
    raw_scores = jnp.dot(features, query_matrix.T, preferred_element_type=jnp.float32)
    full_scores = raw_scores * inv_norm[:, None]
    return jnp.take(full_scores, assignment.astype(jnp.int32), axis=0)
```

```python
import functools

import jax
import jax.numpy as jnp
from jax import lax
from jax.experimental import pallas as pl
from jax.experimental.pallas import tpu as pltpu
from jax.sharding import PartitionSpec as P

LANES = 128
SUB = 8
CHUNK = 32
NT = (((1,), (1,)), ((), ()))


def dot_nt(a, b):
    return lax.dot_general(a, b, NT, preferred_element_type=jnp.float32)


def interleaved(weight):
    k, d = weight.shape
    steps = d // (4 * LANES)
    rows = []
    for c in range(4):
        cols = [weight[:, (4 * j + c) * LANES : (4 * j + c + 1) * LANES] for j in range(steps)]
        rows.append(jnp.concatenate(cols, axis=1))
    return jnp.concatenate(rows, axis=0)


def project(ref, start, size, weight):
    steps = ref.shape[1]
    width = weight.shape[0]
    tiles = [ref[pl.ds(start, size), j].reshape(size * 16, LANES) for j in range(steps)]
    acc = dot_nt(jnp.concatenate(tiles, axis=1), weight).reshape(size, 2, SUB, width)
    lane = lax.broadcasted_iota(jnp.int32, (1, SUB, width), 2) // (width // 4)
    sub = lax.broadcasted_iota(jnp.int32, (1, SUB, width), 1) // 4
    both = jnp.where(lane < 2, acc[:, 0], acc[:, 1])
    both = jnp.where(lane % 2 == sub, both, 0.0)
    both = both + pltpu.roll(both, 4, 1)
    both = both.reshape(size // 2, 2, SUB, width)
    pair = jnp.where(sub == 0, both[:, 0], both[:, 1])
    return pair.reshape(size * 4, width).astype(jnp.bfloat16)


def kernel(
    n,
    layers,
    act_hbm,
    grad_hbm,
    in_hbm,
    out_hbm,
    query_hbm,
    assign_hbm,
    scores_ref,
    act,
    grad,
    w_in,
    w_out,
    query,
    assign,
    spread,
    feats,
    send,
    recv,
    sq_send,
    sq_recv,
    act_sem,
    load_sem,
    send_sem,
    recv_sem,
):
    me = lax.axis_index("section")
    part = lax.axis_index("parts")
    ex = act.shape[0]
    rows = assign.shape[1]
    chunks = ex // CHUNK
    k_in = w_in.shape[0]
    k_out = w_out.shape[0]

    loads = []
    for i, (src, dst) in enumerate(
        ((out_hbm, w_out), (grad_hbm, grad), (in_hbm, w_in))
    ):
        loads.append(pltpu.make_async_copy(src, dst, load_sem.at[i]))
    acts = [
        pltpu.make_async_copy(
            act_hbm.at[pl.ds(i * CHUNK, CHUNK)], act.at[pl.ds(i * CHUNK, CHUNK)], act_sem.at[i]
        )
        for i in range(chunks)
    ]
    late = [
        pltpu.make_async_copy(assign_hbm, assign, load_sem.at[3]),
        pltpu.make_async_copy(query_hbm, query, load_sem.at[4]),
    ]
    late[0].start()
    for copy in loads + acts + late[1:]:
        copy.start()

    barrier = pltpu.get_barrier_semaphore()

    @pl.loop(1, n)
    def _(i):
        pl.semaphore_signal(
            barrier, inc=1, device_id=(part, lax.rem(me + i, n)), device_id_type=pl.DeviceIdType.MESH
        )

    late[0].wait()
    first = (me // layers) * ex
    place = lax.broadcasted_iota(jnp.int32, (4 * ex, rows), 0)
    hot = jnp.where(place == (assign[...] - first) * 4, 1.0, 0.0)
    spread[...] = hot.T.astype(jnp.bfloat16)

    def expander(k, other, of_out):
        src = lax.broadcasted_iota(jnp.int32, (4 * k, k_in * k_out), 0) % k
        dst = lax.broadcasted_iota(jnp.int32, (4 * k, k_in * k_out), 1)
        dst = dst // k_in if of_out else dst % k_in
        return jnp.where(src == dst, 1.0, 0.0).astype(jnp.bfloat16)

    over_out = expander(k_out, k_in, True)
    over_in = expander(k_in, k_out, False)

    loads[0].wait()
    loads[1].wait()
    weight_out = interleaved(w_out[...])
    loads[2].wait()
    weight_in = interleaved(w_in[...])
    for i in range(chunks):
        g = jnp.dot(
            project(grad, i * CHUNK, CHUNK, weight_out), over_out, preferred_element_type=jnp.float32
        )
        acts[i].wait()
        a = jnp.dot(
            project(act, i * CHUNK, CHUNK, weight_in), over_in, preferred_element_type=jnp.float32
        )
        y = (g * a).reshape(CHUNK // 2, SUB, k_in * k_out)
        y = y + pltpu.roll(y, 7, 1)
        y = y + pltpu.roll(y, 6, 1)
        feats[pl.ds(4 * i * CHUNK, 4 * CHUNK), :] = y.reshape(4 * CHUNK, k_in * k_out).astype(
            jnp.bfloat16
        )

    picked = jnp.dot(spread[...], feats[...], preferred_element_type=jnp.float32)
    late[1].wait()
    partial = dot_nt(picked.astype(jnp.bfloat16), query[...])
    blocks = partial.reshape(n, rows // n, partial.shape[1])
    half = blocks.shape[2] // 2
    send[...] = jnp.concatenate([blocks[:, :, :half], blocks[:, :, half:]], axis=1).astype(
        jnp.bfloat16
    )
    square = picked * picked
    folded = square[:, :LANES]
    for j in range(1, square.shape[1] // LANES):
        folded = folded + square[:, j * LANES : (j + 1) * LANES]
    sq_send[...] = jnp.sum(folded.T, axis=0, keepdims=True)

    pl.semaphore_wait(barrier, n - 1)

    def copies(i):
        peer = lax.rem(me + i, n)
        target = dict(device_id=(part, peer), device_id_type=pl.DeviceIdType.MESH)
        return (
            pltpu.make_async_remote_copy(
                send.at[peer], recv.at[i], send_sem.at[0], recv_sem.at[0], **target
            ),
            pltpu.make_async_remote_copy(
                sq_send, sq_recv.at[i], send_sem.at[1], recv_sem.at[1], **target
            ),
        )

    @pl.loop(1, n)
    def _(i):
        for copy in copies(i):
            copy.start()

    pltpu.make_async_copy(recv.at[pl.ds(1, n - 1)], recv.at[pl.ds(1, n - 1)], recv_sem.at[0]).wait()
    pltpu.make_async_copy(
        sq_recv.at[pl.ds(1, n - 1)], sq_recv.at[pl.ds(1, n - 1)], recv_sem.at[1]
    ).wait()
    total = jnp.sum(recv[1:].astype(jnp.float32), axis=0) + send[me].astype(jnp.float32)
    norms = jnp.sum(sq_recv[1:], axis=0) + sq_send[...]
    per = rows // n
    column = lax.broadcasted_iota(jnp.int32, (per, rows), 1)
    mine = column == me * per + lax.broadcasted_iota(jnp.int32, (per, rows), 0)
    norm_sq = jnp.sum(jnp.where(mine, norms, 0.0), axis=1, keepdims=True)
    inv_norm = lax.rsqrt(norm_sq + 1e-06)
    scores_ref[:, :half] = total[:per] * inv_norm
    scores_ref[:, half:] = total[per:] * inv_norm
    pltpu.make_async_copy(send.at[pl.ds(1, n - 1)], send.at[pl.ds(1, n - 1)], send_sem.at[0]).wait()
    pltpu.make_async_copy(
        sq_recv.at[pl.ds(1, n - 1)], sq_recv.at[pl.ds(1, n - 1)], send_sem.at[1]
    ).wait()


def by_register(x):
    ex, tok, d = x.shape
    x = x.reshape(ex, tok, d // (4 * LANES), 4, LANES)
    return x.transpose(0, 2, 3, 1, 4).reshape(ex, d // (4 * LANES), 4 * tok, LANES)


def shards(n, activations, out_grads, in_proj, out_proj, queries, assignment):
    act = by_register(activations[0])
    grad = by_register(out_grads[0])
    rows = assignment.shape[0]
    ex = act.shape[0]
    layers = n // (rows // ex)
    k_in = in_proj.shape[1]
    k_out = out_proj.shape[1]
    any_space = pl.BlockSpec(memory_space=pl.ANY)
    bf16 = jnp.bfloat16
    return pl.pallas_call(
        functools.partial(kernel, n, layers),
        out_shape=jax.ShapeDtypeStruct((rows // n, queries.shape[1]), jnp.float32),
        in_specs=[any_space] * 6,
        out_specs=pl.BlockSpec(memory_space=pltpu.VMEM),
        scratch_shapes=[
            pltpu.VMEM(act.shape, bf16),
            pltpu.VMEM(grad.shape, bf16),
            pltpu.VMEM(in_proj.shape[1:], bf16),
            pltpu.VMEM(out_proj.shape[1:], bf16),
            pltpu.VMEM(queries.shape[1:], bf16),
            pltpu.VMEM((1, rows), jnp.int32),
            pltpu.VMEM((rows, 4 * ex), bf16),
            pltpu.VMEM((4 * ex, k_in * k_out), bf16),
            pltpu.VMEM((n, 16, LANES), bf16),
            pltpu.VMEM((n, 16, LANES), bf16),
            pltpu.VMEM((1, rows), jnp.float32),
            pltpu.VMEM((n, 1, rows), jnp.float32),
            pltpu.SemaphoreType.DMA((ex // CHUNK,)),
            pltpu.SemaphoreType.DMA((5,)),
            pltpu.SemaphoreType.DMA((2,)),
            pltpu.SemaphoreType.DMA((2,)),
        ],
        compiler_params=pltpu.CompilerParams(
            collective_id=0, has_side_effects=True, vmem_limit_bytes=56 * 1024 * 1024
        ),
    )(act, grad, in_proj[0], out_proj[0], queries[0], assignment[None, :])


def solution(mesh):
    return jax.shard_map(
        functools.partial(shards, mesh.shape["section"]),
        mesh=mesh,
        in_specs=(
            P("section", "parts", None, None),
            P("section", "parts", None, None),
            P("section", None, None),
            P("section", None, None),
            P("section", None, None),
            P("parts"),
        ),
        out_specs=P(("parts", "section"), None),
        check_vma=False,
    )
```

```python
import functools

import jax
import jax.numpy as jnp
from jax import lax
from jax.experimental import pallas as pl
from jax.experimental.pallas import tpu as pltpu
from jax.sharding import PartitionSpec as P

LANES = 128
SUB = 8
SHARES = (8,)
NT = (((1,), (1,)), ((), ()))


def dot_nt(a, b):
    return lax.dot_general(a, b, NT, preferred_element_type=jnp.float32)


def interleaved(weight):
    k, d = weight.shape
    steps = d // (4 * LANES)
    rows = []
    for c in range(4):
        cols = [weight[:, (4 * j + c) * LANES : (4 * j + c + 1) * LANES] for j in range(steps)]
        rows.append(jnp.concatenate(cols, axis=1))
    return jnp.concatenate(rows, axis=0)


def project(ref, start, size, weight):
    steps = ref.shape[1]
    width = weight.shape[0]
    tiles = [ref[pl.ds(start, size), j].reshape(size * 16, LANES) for j in range(steps)]
    acc = dot_nt(jnp.concatenate(tiles, axis=1), weight).reshape(size, 2, SUB, width)
    lane = lax.broadcasted_iota(jnp.int32, (1, SUB, width), 2) // (width // 4)
    sub = lax.broadcasted_iota(jnp.int32, (1, SUB, width), 1) // 4
    both = jnp.where(lane < 2, acc[:, 0], acc[:, 1])
    both = jnp.where(lane % 2 == sub, both, 0.0)
    both = both + pltpu.roll(both, 4, 1)
    both = both.reshape(size // 2, 2, SUB, width)
    pair = jnp.where(sub == 0, both[:, 0], both[:, 1])
    return pair.reshape(size * 4, width).astype(jnp.bfloat16)


def kernel(
    n,
    layers,
    act_hbm,
    grad_hbm,
    in_hbm,
    out_hbm,
    query_hbm,
    assign_hbm,
    scores_ref,
    act,
    grad,
    w_in,
    w_out,
    query,
    assign,
    spread,
    wide,
    proj,
    send,
    recv,
    act_sem,
    load_sem,
    send_sem,
    recv_sem,
):
    me = lax.axis_index("section")
    part = lax.axis_index("parts")
    ex = act.shape[0]
    rows = assign.shape[1]
    per = rows // n
    sizes = [ex * share // 8 for share in SHARES]
    starts = [sum(sizes[:i]) for i in range(len(sizes))]
    k_in = w_in.shape[0]
    k_out = w_out.shape[0]

    loads = []
    for i, (src, dst) in enumerate(
        ((out_hbm, w_out), (grad_hbm, grad), (in_hbm, w_in))
    ):
        loads.append(pltpu.make_async_copy(src, dst, load_sem.at[i]))
    acts = [
        pltpu.make_async_copy(
            act_hbm.at[pl.ds(at, size)], act.at[pl.ds(at, size)], act_sem.at[i]
        )
        for i, (at, size) in enumerate(zip(starts, sizes))
    ]
    late = [
        pltpu.make_async_copy(assign_hbm, assign, load_sem.at[3]),
        pltpu.make_async_copy(query_hbm, query, load_sem.at[4]),
    ]
    late[0].start()
    for copy in loads + acts + late[1:]:
        copy.start()

    barrier = pltpu.get_barrier_semaphore()

    @pl.loop(1, n)
    def _(i):
        pl.semaphore_signal(
            barrier, inc=1, device_id=(part, lax.rem(me + i, n)), device_id_type=pl.DeviceIdType.MESH
        )

    late[0].wait()
    first = (me // layers) * ex
    place = lax.broadcasted_iota(jnp.int32, (4 * ex, rows), 0)
    hot = jnp.where(place == (assign[...] - first) * 4, 1.0, 0.0)
    spread[...] = hot.T.astype(jnp.bfloat16)

    def expander(k, other, of_out):
        src = lax.broadcasted_iota(jnp.int32, (4 * k, k_in * k_out), 0) % k
        dst = lax.broadcasted_iota(jnp.int32, (4 * k, k_in * k_out), 1)
        dst = dst // k_in if of_out else dst % k_in
        return jnp.where(src == dst, 1.0, 0.0).astype(jnp.bfloat16)

    over_out = expander(k_out, k_in, True)
    over_in = expander(k_in, k_out, False)

    loads[0].wait()
    loads[2].wait()
    weight_in = interleaved(w_in[...])
    weight_out = interleaved(w_out[...])
    loads[1].wait()
    wide[...] = jnp.dot(
        project(grad, 0, ex, weight_out), over_out, preferred_element_type=jnp.float32
    )
    for i, (at, size) in enumerate(zip(starts, sizes)):
        acts[i].wait()
        proj[pl.ds(4 * at, 4 * size), :] = project(act, at, size, weight_in)
    late[1].wait()
    y = wide[...] * jnp.dot(proj[...], over_in, preferred_element_type=jnp.float32)
    y = y.reshape(ex // 2, SUB, k_in * k_out)
    y = y + pltpu.roll(y, 7, 1)
    y = y + pltpu.roll(y, 6, 1)
    features = y.reshape(4 * ex, k_in * k_out).astype(jnp.bfloat16)

    picked = jnp.dot(spread[...], features, preferred_element_type=jnp.float32)
    partial = dot_nt(picked.astype(jnp.bfloat16), query[...])
    blocks = partial.reshape(n, per, partial.shape[1])
    half = blocks.shape[2] // 2
    square = jnp.sum(picked * picked, axis=1, keepdims=True)
    square = jnp.broadcast_to(square, (rows, LANES)).reshape(n, per, LANES)
    high = square.astype(jnp.bfloat16).astype(jnp.float32)
    send[...] = jnp.concatenate(
        [blocks[:, :, :half], blocks[:, :, half:], high, square - high], axis=1
    ).astype(jnp.bfloat16)

    pl.semaphore_wait(barrier, n - 1)

    @pl.loop(1, n)
    def _(i):
        peer = lax.rem(me + i, n)
        pltpu.make_async_remote_copy(
            send.at[peer],
            recv.at[i],
            send_sem,
            recv_sem,
            device_id=(part, peer),
            device_id_type=pl.DeviceIdType.MESH,
        ).start()

    others = pl.ds(1, n - 1)
    pltpu.make_async_copy(recv.at[others], recv.at[others], recv_sem).wait()
    total = jnp.sum(recv[1:].astype(jnp.float32), axis=0) + send[me].astype(jnp.float32)
    inv_norm = lax.rsqrt(total[2 * per : 3 * per] + total[3 * per :] + 1e-06)
    scores_ref[:, :half] = total[:per] * inv_norm
    scores_ref[:, half:] = total[per : 2 * per] * inv_norm
    pltpu.make_async_copy(send.at[others], send.at[others], send_sem).wait()


def by_register(x):
    ex, tok, d = x.shape
    x = x.reshape(ex, tok, d // (4 * LANES), 4, LANES)
    return x.transpose(0, 2, 3, 1, 4).reshape(ex, d // (4 * LANES), 4 * tok, LANES)


def shards(n, activations, out_grads, in_proj, out_proj, queries, assignment):
    act = by_register(activations[0])
    grad = by_register(out_grads[0])
    rows = assignment.shape[0]
    ex = act.shape[0]
    layers = n // (rows // ex)
    k_in = in_proj.shape[1]
    k_out = out_proj.shape[1]
    any_space = pl.BlockSpec(memory_space=pl.ANY)
    bf16 = jnp.bfloat16
    return pl.pallas_call(
        functools.partial(kernel, n, layers),
        out_shape=pltpu.VMEM((rows // n, queries.shape[1]), jnp.float32),
        in_specs=[any_space] * 6,
        out_specs=pl.BlockSpec(memory_space=pltpu.VMEM),
        scratch_shapes=[
            pltpu.VMEM(act.shape, bf16),
            pltpu.VMEM(grad.shape, bf16),
            pltpu.VMEM(in_proj.shape[1:], bf16),
            pltpu.VMEM(out_proj.shape[1:], bf16),
            pltpu.VMEM(queries.shape[1:], bf16),
            pltpu.VMEM((1, rows), jnp.int32),
            pltpu.VMEM((rows, 4 * ex), bf16),
            pltpu.VMEM((4 * ex, k_in * k_out), jnp.float32),
            pltpu.VMEM((4 * ex, 4 * k_in), bf16),
            pltpu.VMEM((n, 4 * (rows // n), LANES), bf16),
            pltpu.VMEM((n, 4 * (rows // n), LANES), bf16),
            pltpu.SemaphoreType.DMA((len(SHARES),)),
            pltpu.SemaphoreType.DMA((5,)),
            pltpu.SemaphoreType.DMA,
            pltpu.SemaphoreType.DMA,
        ],
        compiler_params=pltpu.CompilerParams(
            collective_id=0, has_side_effects=True, vmem_limit_bytes=56 * 1024 * 1024
        ),
    )(act, grad, in_proj[0], out_proj[0], queries[0], assignment[None, :])


def solution(mesh):
    return jax.shard_map(
        functools.partial(shards, mesh.shape["section"]),
        mesh=mesh,
        in_specs=(
            P("section", "parts", None, None),
            P("section", "parts", None, None),
            P("section", None, None),
            P("section", None, None),
            P("section", None, None),
            P("parts"),
        ),
        out_specs=P(("parts", "section"), None),
        check_vma=False,
    )
```

```python
import functools

import jax
import jax.numpy as jnp
from jax import lax
from jax.experimental import pallas as pl
from jax.experimental.pallas import tpu as pltpu
from jax.sharding import PartitionSpec as P

LANES = 128
SUB = 8
ACT_STEP = 64
GRAD_STEP = 32
NT = (((1,), (1,)), ((), ()))


def dot_nt(a, b):
    return lax.dot_general(a, b, NT, preferred_element_type=jnp.float32)


def interleaved(weight):
    k, d = weight.shape
    steps = d // (4 * LANES)
    rows = []
    for c in range(4):
        cols = [weight[:, (4 * j + c) * LANES : (4 * j + c + 1) * LANES] for j in range(steps)]
        rows.append(jnp.concatenate(cols, axis=1))
    return jnp.concatenate(rows, axis=0)


def project(ref, start, size, weight):
    steps = ref.shape[1]
    width = weight.shape[0]
    tiles = [ref[pl.ds(start, size), j].reshape(size * 16, LANES) for j in range(steps)]
    acc = dot_nt(jnp.concatenate(tiles, axis=1), weight).reshape(size, 2, SUB, width)
    lane = lax.broadcasted_iota(jnp.int32, (1, SUB, width), 2) // (width // 4)
    sub = lax.broadcasted_iota(jnp.int32, (1, SUB, width), 1) // 4
    both = jnp.where(lane < 2, acc[:, 0], acc[:, 1])
    both = jnp.where(lane % 2 == sub, both, 0.0)
    both = both + pltpu.roll(both, 4, 1)
    both = both.reshape(size // 2, 2, SUB, width)
    pair = jnp.where(sub == 0, both[:, 0], both[:, 1])
    return pair.reshape(size * 4, width).astype(jnp.bfloat16)


def kernel(
    n,
    layers,
    act_hbm,
    grad_hbm,
    in_hbm,
    out_hbm,
    query_hbm,
    assign_hbm,
    scores_ref,
    act,
    grad,
    w_in,
    w_out,
    query,
    assign,
    spread,
    wide,
    proj,
    send,
    recv,
    load_sem,
    send_sem,
    recv_sem,
):
    me = lax.axis_index("section")
    part = lax.axis_index("parts")
    ex = act.shape[0]
    rows = assign.shape[1]
    per = rows // n
    k_in = w_in.shape[0]
    k_out = w_out.shape[0]

    loads = []
    for i, (src, dst) in enumerate(
        ((out_hbm, w_out), (grad_hbm, grad), (in_hbm, w_in), (act_hbm, act))
    ):
        loads.append(pltpu.make_async_copy(src, dst, load_sem.at[i]))
    late = [
        pltpu.make_async_copy(assign_hbm, assign, load_sem.at[4]),
        pltpu.make_async_copy(query_hbm, query, load_sem.at[5]),
    ]
    late[0].start()
    for copy in loads + late[1:]:
        copy.start()

    barrier = pltpu.get_barrier_semaphore()

    @pl.loop(1, n)
    def _(i):
        pl.semaphore_signal(
            barrier, inc=1, device_id=(part, lax.rem(me + i, n)), device_id_type=pl.DeviceIdType.MESH
        )

    late[0].wait()
    first = (me // layers) * ex
    place = lax.broadcasted_iota(jnp.int32, (4 * ex, rows), 0)
    hot = jnp.where(place == (assign[...] - first) * 4, 1.0, 0.0)
    spread[...] = hot.T.astype(jnp.bfloat16)

    def expander(k, other, of_out):
        src = lax.broadcasted_iota(jnp.int32, (4 * k, k_in * k_out), 0) % k
        dst = lax.broadcasted_iota(jnp.int32, (4 * k, k_in * k_out), 1)
        dst = dst // k_in if of_out else dst % k_in
        return jnp.where(src == dst, 1.0, 0.0).astype(jnp.bfloat16)

    over_out = expander(k_out, k_in, True)
    over_in = expander(k_in, k_out, False)

    loads[0].wait()
    loads[2].wait()
    weight_in = interleaved(w_in[...])
    weight_out = interleaved(w_out[...])
    loads[1].wait()
    for at in range(0, ex, GRAD_STEP):
        wide[pl.ds(4 * at, 4 * GRAD_STEP), :] = jnp.dot(
            project(grad, at, GRAD_STEP, weight_out), over_out, preferred_element_type=jnp.float32
        )
    loads[3].wait()
    for at in range(0, ex, ACT_STEP):
        proj[pl.ds(4 * at, 4 * ACT_STEP), :] = project(act, at, ACT_STEP, weight_in)
    late[1].wait()
    y = wide[...] * jnp.dot(proj[...], over_in, preferred_element_type=jnp.float32)
    y = y.reshape(ex // 2, SUB, k_in * k_out)
    y = y + pltpu.roll(y, 7, 1)
    y = y + pltpu.roll(y, 6, 1)
    features = y.reshape(4 * ex, k_in * k_out).astype(jnp.bfloat16)

    picked = jnp.dot(spread[...], features, preferred_element_type=jnp.float32)
    partial = dot_nt(picked.astype(jnp.bfloat16), query[...])
    blocks = partial.reshape(n, per, partial.shape[1])
    half = blocks.shape[2] // 2
    square = jnp.sum(picked * picked, axis=1, keepdims=True)
    square = jnp.broadcast_to(square, (rows, LANES)).reshape(n, per, LANES)
    high = square.astype(jnp.bfloat16).astype(jnp.float32)
    send[...] = jnp.concatenate(
        [blocks[:, :, :half], blocks[:, :, half:], high, square - high], axis=1
    ).astype(jnp.bfloat16)

    pl.semaphore_wait(barrier, n - 1)

    @pl.loop(1, n)
    def _(i):
        peer = lax.rem(me + i, n)
        pltpu.make_async_remote_copy(
            send.at[peer],
            recv.at[i],
            send_sem,
            recv_sem,
            device_id=(part, peer),
            device_id_type=pl.DeviceIdType.MESH,
        ).start()

    others = pl.ds(1, n - 1)
    pltpu.make_async_copy(recv.at[others], recv.at[others], recv_sem).wait()
    total = jnp.sum(recv[1:].astype(jnp.float32), axis=0) + send[me].astype(jnp.float32)
    inv_norm = lax.rsqrt(total[2 * per : 3 * per] + total[3 * per :] + 1e-06)
    scores_ref[:, :half] = total[:per] * inv_norm
    scores_ref[:, half:] = total[per : 2 * per] * inv_norm
    pltpu.make_async_copy(send.at[others], send.at[others], send_sem).wait()


def by_register(x):
    ex, tok, d = x.shape
    x = x.reshape(ex, tok, d // (4 * LANES), 4, LANES)
    return x.transpose(0, 2, 3, 1, 4).reshape(ex, d // (4 * LANES), 4 * tok, LANES)


def shards(n, activations, out_grads, in_proj, out_proj, queries, assignment):
    act = by_register(activations[0])
    grad = by_register(out_grads[0])
    rows = assignment.shape[0]
    ex = act.shape[0]
    layers = n // (rows // ex)
    k_in = in_proj.shape[1]
    k_out = out_proj.shape[1]
    any_space = pl.BlockSpec(memory_space=pl.ANY)
    bf16 = jnp.bfloat16
    return pl.pallas_call(
        functools.partial(kernel, n, layers),
        out_shape=pltpu.VMEM((rows // n, queries.shape[1]), jnp.float32),
        in_specs=[any_space] * 6,
        out_specs=pl.BlockSpec(memory_space=pltpu.VMEM),
        scratch_shapes=[
            pltpu.VMEM(act.shape, bf16),
            pltpu.VMEM(grad.shape, bf16),
            pltpu.VMEM(in_proj.shape[1:], bf16),
            pltpu.VMEM(out_proj.shape[1:], bf16),
            pltpu.VMEM(queries.shape[1:], bf16),
            pltpu.VMEM((1, rows), jnp.int32),
            pltpu.VMEM((rows, 4 * ex), bf16),
            pltpu.VMEM((4 * ex, k_in * k_out), jnp.float32),
            pltpu.VMEM((4 * ex, 4 * k_in), bf16),
            pltpu.VMEM((n, 4 * (rows // n), LANES), bf16),
            pltpu.VMEM((n, 4 * (rows // n), LANES), bf16),
            pltpu.SemaphoreType.DMA((6,)),
            pltpu.SemaphoreType.DMA,
            pltpu.SemaphoreType.DMA,
        ],
        compiler_params=pltpu.CompilerParams(
            collective_id=0, has_side_effects=True, vmem_limit_bytes=56 * 1024 * 1024
        ),
    )(act, grad, in_proj[0], out_proj[0], queries[0], assignment[None, :])


def solution(mesh):
    return jax.shard_map(
        functools.partial(shards, mesh.shape["section"]),
        mesh=mesh,
        in_specs=(
            P("section", "parts", None, None),
            P("section", "parts", None, None),
            P("section", None, None),
            P("section", None, None),
            P("section", None, None),
            P("parts"),
        ),
        out_specs=P(("parts", "section"), None),
        check_vma=False,
    )
```

```python
import functools

import jax
import jax.numpy as jnp
from jax import lax
from jax.experimental import pallas as pl
from jax.experimental.pallas import tpu as pltpu
from jax.sharding import PartitionSpec as P

LANES = 128
SUB = 8
ACT_STEP = 64
GRAD_STEP = 32
NT = (((1,), (1,)), ((), ()))


def dot_nt(a, b):
    return lax.dot_general(a, b, NT, preferred_element_type=jnp.float32)


def interleaved(weight):
    k, d = weight.shape
    steps = d // (4 * LANES)
    rows = []
    for c in range(4):
        cols = [weight[:, (4 * j + c) * LANES : (4 * j + c + 1) * LANES] for j in range(steps)]
        rows.append(jnp.concatenate(cols, axis=1))
    return jnp.concatenate(rows, axis=0)


def project(ref, start, size, weight):
    steps = ref.shape[1]
    width = weight.shape[0]
    tiles = [ref[pl.ds(start, size), j].reshape(size * 16, LANES) for j in range(steps)]
    acc = dot_nt(jnp.concatenate(tiles, axis=1), weight).reshape(size, 2, SUB, width)
    lane = lax.broadcasted_iota(jnp.int32, (1, SUB, width), 2) // (width // 4)
    sub = lax.broadcasted_iota(jnp.int32, (1, SUB, width), 1) // 4
    both = jnp.where(lane < 2, acc[:, 0], acc[:, 1])
    both = jnp.where(lane % 2 == sub, both, 0.0)
    both = both + pltpu.roll(both, 4, 1)
    both = both.reshape(size // 2, 2, SUB, width)
    pair = jnp.where(sub == 0, both[:, 0], both[:, 1])
    return pair.reshape(size * 4, width).astype(jnp.bfloat16)


def kernel(
    n,
    layers,
    act_hbm,
    grad_hbm,
    in_hbm,
    out_hbm,
    query_hbm,
    assign_hbm,
    scores_ref,
    act,
    grad,
    w_in,
    w_out,
    query,
    assign,
    spread,
    wide,
    proj,
    send,
    recv,
    load_sem,
    send_sem,
    recv_sem,
):
    me = lax.axis_index("section")
    part = lax.axis_index("parts")
    ex = act.shape[0]
    rows = assign.shape[1]
    per = rows // n
    k_in = w_in.shape[0]
    k_out = w_out.shape[0]

    loads = []
    for i, (src, dst) in enumerate(
        ((out_hbm, w_out), (grad_hbm, grad), (in_hbm, w_in), (act_hbm, act))
    ):
        loads.append(pltpu.make_async_copy(src, dst, load_sem.at[i]))
    late = [
        pltpu.make_async_copy(assign_hbm, assign, load_sem.at[4]),
        pltpu.make_async_copy(query_hbm, query, load_sem.at[5]),
    ]
    late[0].start()
    for copy in loads + late[1:]:
        copy.start()

    barrier = pltpu.get_barrier_semaphore()

    @pl.loop(1, n)
    def _(i):
        pl.semaphore_signal(
            barrier, inc=1, device_id=(part, lax.rem(me + i, n)), device_id_type=pl.DeviceIdType.MESH
        )

    late[0].wait()
    first = (me // layers) * ex
    place = lax.broadcasted_iota(jnp.int32, (4 * ex, rows), 0)
    hot = jnp.where(place == (assign[...] - first) * 4, 1.0, 0.0)
    spread[...] = hot.T.astype(jnp.bfloat16)

    def expander(k, other, of_out):
        src = lax.broadcasted_iota(jnp.int32, (4 * k, k_in * k_out), 0) % k
        dst = lax.broadcasted_iota(jnp.int32, (4 * k, k_in * k_out), 1)
        dst = dst // k_in if of_out else dst % k_in
        return jnp.where(src == dst, 1.0, 0.0).astype(jnp.bfloat16)

    over_out = expander(k_out, k_in, True)
    over_in = expander(k_in, k_out, False)

    loads[0].wait()
    weight_out = interleaved(w_out[...])
    loads[1].wait()
    for at in range(0, ex, GRAD_STEP):
        wide[pl.ds(4 * at, 4 * GRAD_STEP), :] = jnp.dot(
            project(grad, at, GRAD_STEP, weight_out), over_out, preferred_element_type=jnp.float32
        )
    loads[2].wait()
    weight_in = interleaved(w_in[...])
    loads[3].wait()
    for at in range(0, ex, ACT_STEP):
        proj[pl.ds(4 * at, 4 * ACT_STEP), :] = project(act, at, ACT_STEP, weight_in)
    late[1].wait()
    y = wide[...] * jnp.dot(proj[...], over_in, preferred_element_type=jnp.float32)
    y = y.reshape(ex // 2, SUB, k_in * k_out)
    y = y + pltpu.roll(y, 7, 1)
    y = y + pltpu.roll(y, 6, 1)
    features = y.reshape(4 * ex, k_in * k_out).astype(jnp.bfloat16)

    picked = jnp.dot(spread[...], features, preferred_element_type=jnp.float32)
    partial = dot_nt(picked.astype(jnp.bfloat16), query[...])
    blocks = partial.reshape(n, per, partial.shape[1])
    half = blocks.shape[2] // 2
    square = jnp.sum(picked * picked, axis=1, keepdims=True)
    square = jnp.broadcast_to(square, (rows, LANES)).reshape(n, per, LANES)
    high = square.astype(jnp.bfloat16).astype(jnp.float32)
    send[...] = jnp.concatenate(
        [blocks[:, :, :half], blocks[:, :, half:], high, square - high], axis=1
    ).astype(jnp.bfloat16)

    pl.semaphore_wait(barrier, n - 1)

    @pl.loop(1, n)
    def _(i):
        peer = lax.rem(me + i, n)
        pltpu.make_async_remote_copy(
            send.at[peer],
            recv.at[i],
            send_sem,
            recv_sem,
            device_id=(part, peer),
            device_id_type=pl.DeviceIdType.MESH,
        ).start()

    others = pl.ds(1, n - 1)
    pltpu.make_async_copy(recv.at[others], recv.at[others], recv_sem).wait()
    total = jnp.sum(recv[1:].astype(jnp.float32), axis=0) + send[me].astype(jnp.float32)
    inv_norm = lax.rsqrt(total[2 * per : 3 * per] + total[3 * per :] + 1e-06)
    scores_ref[:, :half] = total[:per] * inv_norm
    scores_ref[:, half:] = total[per : 2 * per] * inv_norm
    pltpu.make_async_copy(send.at[others], send.at[others], send_sem).wait()


def by_register(x):
    ex, tok, d = x.shape
    x = x.reshape(ex, tok, d // (4 * LANES), 4, LANES)
    return x.transpose(0, 2, 3, 1, 4).reshape(ex, d // (4 * LANES), 4 * tok, LANES)


def shards(n, activations, out_grads, in_proj, out_proj, queries, assignment):
    act = by_register(activations[0])
    grad = by_register(out_grads[0])
    rows = assignment.shape[0]
    ex = act.shape[0]
    layers = n // (rows // ex)
    k_in = in_proj.shape[1]
    k_out = out_proj.shape[1]
    any_space = pl.BlockSpec(memory_space=pl.ANY)
    bf16 = jnp.bfloat16
    return pl.pallas_call(
        functools.partial(kernel, n, layers),
        out_shape=pltpu.VMEM((rows // n, queries.shape[1]), jnp.float32),
        in_specs=[any_space] * 6,
        out_specs=pl.BlockSpec(memory_space=pltpu.VMEM),
        scratch_shapes=[
            pltpu.VMEM(act.shape, bf16),
            pltpu.VMEM(grad.shape, bf16),
            pltpu.VMEM(in_proj.shape[1:], bf16),
            pltpu.VMEM(out_proj.shape[1:], bf16),
            pltpu.VMEM(queries.shape[1:], bf16),
            pltpu.VMEM((1, rows), jnp.int32),
            pltpu.VMEM((rows, 4 * ex), bf16),
            pltpu.VMEM((4 * ex, k_in * k_out), jnp.float32),
            pltpu.VMEM((4 * ex, 4 * k_in), bf16),
            pltpu.VMEM((n, 4 * (rows // n), LANES), bf16),
            pltpu.VMEM((n, 4 * (rows // n), LANES), bf16),
            pltpu.SemaphoreType.DMA((6,)),
            pltpu.SemaphoreType.DMA,
            pltpu.SemaphoreType.DMA,
        ],
        compiler_params=pltpu.CompilerParams(
            collective_id=0, has_side_effects=True, vmem_limit_bytes=56 * 1024 * 1024
        ),
    )(act, grad, in_proj[0], out_proj[0], queries[0], assignment[None, :])


def solution(mesh):
    return jax.shard_map(
        functools.partial(shards, mesh.shape["section"]),
        mesh=mesh,
        in_specs=(
            P("section", "parts", None, None),
            P("section", "parts", None, None),
            P("section", None, None),
            P("section", None, None),
            P("section", None, None),
            P("parts"),
        ),
        out_specs=P(("parts", "section"), None),
        check_vma=False,
    )
```
